32 devices in a mesh: dp: 8 (over z, core), proto: 4 (over y, x).
Axes of the slice: x: 2, y: 2, z: 4, core: 2. Of those that a mesh axis runs over, the one named last changes fastest.
Arguments:
- student_rows: bfloat16 [32, 256, 256], P('dp'), may hold values from -8 to 8
- teacher_rows: bfloat16 [32, 256, 256], P('dp'), may hold values from -8 to 8
- prototypes: bfloat16 [256, 131072], P(None, 'proto'), may hold values from -8 to 8
- center: float32 [131072], P('proto'), may hold values from -1.2 to 1.2
- mask_index: int32 [32, 128], P('dp'), may hold values from 0 to 255, as said below
- mask_count: int32 [32], P('dp'), may hold values from 0 to 128, as said below
- loss_scale: float32 [], replicated, may hold values from 1024 to 4096
Outputs:
- loss: float32 [], replicated
- student_grad: float32 [32, 256, 256], P('dp')
- proto_grad: float32 [131072, 256], P(('proto', 'dp'))
- patch_center: float32 [131072], P('proto')
The draws below stay inside these ranges and needn't reach their ends.
Inputs may be any that keep to these rules, and one draw needn't show every extreme that they name: `mask_index`: for each image the first mask_count entries are distinct patch numbers; the later entries are patch numbers that are ignored. `mask_count`: the counts of all 32 images sum to 2048; some images have no masked patch.
All inputs are finite; a program needn't handle non-finite values.
Results may differ from the reference program's by a relative error of at most 0.022.
Values may be sent and summed in bfloat16 or wider, within the bound.
A program may use at most 256 MiB of HBM per device.

```python
import math
import jax
import jax.numpy as jnp
from jax import lax

D = 256
PROTOS = 131072
PATCHES = 256
MAXM = 128
IMAGES = 32
TOTAL = 2048


def draw_prototypes(key, part):
    key = jax.random.fold_in(key, 21)
    base = 0.5 * jax.random.normal(key, (D, PROTOS), jnp.float32)
    return jnp.clip(base, -8.0, 8.0).astype(jnp.bfloat16)


def draw_student_rows(key, part):
    key = jax.random.fold_in(key, 31)
    first = jax.random.fold_in(key, 0)
    base = jax.random.normal(first, (IMAGES, PATCHES, D), jnp.float32)
    return jnp.clip(base, -8.0, 8.0).astype(jnp.bfloat16)


def draw_teacher_rows(key, part):
    key = jax.random.fold_in(key, 41)
    first = jax.random.fold_in(key, 0)
    fourth = jax.random.fold_in(key, 3)
    shared = jax.random.normal(fourth, (1, 1, D), jnp.float32)
    base = 0.7 * jax.random.normal(first, (IMAGES, PATCHES, D), jnp.float32) + 0.7 * shared
    return jnp.clip(base, -8.0, 8.0).astype(jnp.bfloat16)


def draw_mask_index(key, part):
    key = jax.random.fold_in(key, 13)
    keys = jax.random.split(key, IMAGES)
    orders = jax.vmap(lambda single: jax.random.permutation(single, PATCHES))(keys)
    return orders[:, :MAXM].astype(jnp.int32)


def draw_mask_count(key, part):
    key = jax.random.fold_in(key, 11)
    first, second, third = jax.random.split(key, 3)
    half = IMAGES // 2
    counts = jax.random.randint(first, (half,), 0, MAXM + 1)
    masked = jax.random.randint(third, (half,), 0, 2)
    counts = (counts * masked).at[0].set(0)
    full = jnp.concatenate([counts, MAXM - counts])
    order = jax.random.permutation(second, IMAGES)
    return full[order].astype(jnp.int32)


def levels(key, shape, shards, low, high):
    loudness = 1.0
    for dim, shards_of in shards:
        steps = jax.random.uniform(jax.random.fold_in(jax.random.fold_in(key, 6), dim), (shards_of,), jnp.float32, low / len(shards), high / len(shards))
        loudness = loudness * jnp.repeat(jnp.exp(steps), shape[dim] // shards_of).reshape((-1,) + (1,) * (len(shape) - 1 - dim))
    return loudness


def centred(stream_key, dims, deviation, most, shards=(), kind=jnp.bfloat16):
    values = jax.random.normal(stream_key, dims, jnp.float32) * deviation
    if len(shards) > 0:
        values = levels(stream_key, dims, shards, -0.22, 0.18) * values
    return jnp.clip(values, min=-most, max=most).astype(kind)


def setup_inputs(seed: int = 0) -> dict:
    seeds = jax.random.split(jax.random.key(seed), 8)
    student_rows = draw_student_rows(jax.random.fold_in(seeds[7], 71), 0)
    teacher_rows = draw_teacher_rows(jax.random.fold_in(seeds[7], 71), 0)
    prototypes = draw_prototypes(jax.random.fold_in(seeds[7], 71), 0)
    center = centred(seeds[3], (PROTOS,), 0.2, 1.2, ((0, 4),), jnp.float32)
    mask_index = draw_mask_index(jax.random.fold_in(seeds[7], 71), 0)
    mask_count = draw_mask_count(jax.random.fold_in(seeds[7], 71), 0)
    loss_scale = jnp.clip(jnp.exp(jax.random.uniform(seeds[6], (), jnp.float32, math.log(1024.0), math.log(4096.0))), 1024.0, 4096.0)
    return {"student_rows": student_rows, "teacher_rows": teacher_rows, "prototypes": prototypes, "center": center, "mask_index": mask_index, "mask_count": mask_count, "loss_scale": loss_scale}


teacher_temp = 0.04
student_temp = 0.1
norm_epsilon = 1e-06

def unit_rows(raw):
    values = raw.astype(jnp.float32)
    length = jnp.sqrt(lax.optimization_barrier(jnp.sum(values * values, axis=1, keepdims=True)) + norm_epsilon)
    return (values / length, length)

def reference(student_rows, teacher_rows, prototypes, center, mask_index, mask_count, loss_scale):
    ends = jnp.cumsum(mask_count).astype(jnp.int32)
    starts = (ends - mask_count).astype(jnp.int32)
    rank = jnp.arange(TOTAL, dtype=jnp.int32)
    image = lax.optimization_barrier(jnp.sum((ends[None, :] <= rank[:, None]).astype(jnp.int32), axis=1)).astype(jnp.int32)
    within = (rank - starts[image]).astype(jnp.int32)
    patch = mask_index[image, within].astype(jnp.int32)
    weight = 1.0 / (IMAGES * mask_count[image].astype(jnp.float32))
    block = min(TOTAL, 512)
    blocks = TOTAL // block

    def one_block(carry, item):
        loss_sum, col_sum, grad_sum = carry
        img_b, patch_b, weight_b = item
        s_unit, s_len = unit_rows(student_rows[img_b, patch_b])
        t_unit, t_len = unit_rows(teacher_rows[img_b, patch_b])
        s_half = s_unit.astype(jnp.bfloat16)
        t_half = t_unit.astype(jnp.bfloat16)
        s_logit = jnp.dot(s_half, prototypes, preferred_element_type=jnp.float32)
        t_logit = jnp.dot(t_half, prototypes, preferred_element_type=jnp.float32)
        col_sum = col_sum + lax.optimization_barrier(jnp.sum(t_logit, axis=0))
        t_prob = jax.nn.softmax((t_logit - center[None, :]) / teacher_temp, axis=1)
        s_arg = s_logit / student_temp
        s_lse = jax.nn.logsumexp(s_arg, axis=1)
        s_prob = jnp.exp(s_arg - s_lse[:, None])
        ce = s_lse - lax.optimization_barrier(jnp.sum(t_prob * s_arg, axis=1))
        loss_sum = loss_sum + jnp.sum(weight_b * ce)
        dlogit = (loss_scale * weight_b[:, None] * (s_prob - t_prob) / student_temp).astype(jnp.bfloat16)
        d_unit = jnp.dot(dlogit, prototypes.T, preferred_element_type=jnp.float32)
        grad_sum = grad_sum + jnp.dot(dlogit.T, s_half, preferred_element_type=jnp.float32)
        row_grad = (d_unit - s_unit * lax.optimization_barrier(jnp.sum(s_unit * d_unit, axis=1, keepdims=True))) / s_len
        return ((loss_sum, col_sum, grad_sum), row_grad)
    init = (jnp.zeros((), jnp.float32), jnp.zeros((PROTOS,), jnp.float32), jnp.zeros((PROTOS, D), jnp.float32))
    items = (image.reshape(blocks, block), patch.reshape(blocks, block), weight.reshape(blocks, block))
    (loss, col_sum, proto_grad), row_grads = lax.scan(one_block, init, items)
    row_grads = row_grads.reshape(TOTAL, D)
    student_grad = jnp.zeros((IMAGES, PATCHES, D), jnp.float32).at[image, patch].set(row_grads)
    patch_center = col_sum / TOTAL
    return (loss, student_grad, proto_grad, patch_center)
```

```python
import functools
import math

import jax
import jax.numpy as jnp
from jax import lax
from jax.experimental import pallas as pl
from jax.experimental.pallas import tpu as pltpu
from jax.sharding import PartitionSpec as P

teacher_temp = 0.04
student_temp = 0.1
norm_epsilon = 1e-06
log2_e = math.log2(math.e)
ln_2 = math.log(2.0)
tail_rows = 16
vmem_bytes = 56 * 1024 * 1024
f32 = jnp.float32
bf16 = jnp.bfloat16


def unit_rows(raw):
    values = raw.astype(f32)
    length = jnp.sqrt(jnp.sum(values * values, axis=1, keepdims=True) + norm_epsilon)
    return (values / length, length)


def norm_backward(d_unit, s_unit, s_len):
    return (d_unit - s_unit * jnp.sum(s_unit * d_unit, axis=1, keepdims=True)) / s_len


def compact_kernel(max_masked, starts_ref, rows_ref, s_ref, t_ref, held):
    devices, piece, both = rows_ref.shape
    piece -= tail_rows
    total, width = s_ref.shape
    chunk = min(piece, max_masked)

    @pl.loop(0, devices * piece // chunk)
    def _(step):
        flat = step * chunk
        image = flat // max_masked
        at = starts_ref[image] + flat % max_masked
        row = pl.multiple_of(flat % piece, chunk)
        base = pl.multiple_of(at // 8 * 8, 8)
        ahead = at - base
        value = rows_ref[flat // piece, pl.ds(row, chunk), :].astype(f32)
        value = jnp.concatenate([value, jnp.zeros((8, both), f32)], axis=0)
        value = pltpu.roll(value, ahead, 0)
        older = lax.broadcasted_iota(jnp.int32, (8, both), 0) < ahead
        held[pl.ds(base, 8), :] = jnp.where(older, held[pl.ds(base, 8), :], value[:8])
        held[pl.ds(pl.multiple_of(base + 8, 8), chunk), :] = value[8:]

    s_ref[...] = held[:total, :width].astype(bf16)
    t_ref[...] = held[:total, width:].astype(bf16)


def compact(rows, starts, max_masked, total, width):
    return pl.pallas_call(
        functools.partial(compact_kernel, max_masked),
        out_shape=[jax.ShapeDtypeStruct((total, width), bf16)] * 2,
        in_specs=[
            pl.BlockSpec(memory_space=pltpu.SMEM),
            pl.BlockSpec(memory_space=pltpu.VMEM),
        ],
        out_specs=[pl.BlockSpec(memory_space=pltpu.VMEM)] * 2,
        scratch_shapes=[pltpu.VMEM((total + max_masked + 8, 2 * width), f32)],
        compiler_params=pltpu.CompilerParams(vmem_limit_bytes=vmem_bytes),
        name="compact_rows",
    )(starts, rows)


def nt_dot(left, right):
    return lax.dot_general(left, right, (((1,), (1,)), ((), ())), preferred_element_type=f32)


def forward_kernel(s_ref, t_ref, pt_ref, p_ref, c_ref, us_ref, ut_ref, as_ref, at_ref, stat_ref, s_arg, t_arg):
    cols, rows = s_arg.shape
    width = p_ref.shape[0]
    chunk = min(512, cols)
    chunks = [pl.ds(k * chunk, chunk) for k in range(cols // chunk)]
    s_rows = s_ref[...]
    t_rows = t_ref[...]
    lanes = c_ref.shape[1]

    def fold(value):
        return value.reshape(chunk // 8, 8, rows)

    t_top = jnp.full((8, rows), -jnp.inf, f32)
    for part in chunks:
        shift = jnp.concatenate([c_ref[part, :]] * (rows // lanes), axis=1)
        arg = nt_dot(pt_ref[part, :], t_rows) * (log2_e / teacher_temp) - shift
        t_arg[part, :] = arg
        t_top = jnp.maximum(t_top, jnp.max(fold(arg), axis=0))
    t_top = jnp.max(t_top, axis=0, keepdims=True)

    s_top = jnp.full((8, rows), -jnp.inf, f32)
    t_sum = jnp.zeros((8, rows), f32)
    t_acc = jnp.zeros((width, rows), f32)
    for part in chunks:
        arg = nt_dot(pt_ref[part, :], s_rows) * (log2_e / student_temp)
        s_arg[part, :] = arg
        s_top = jnp.maximum(s_top, jnp.max(fold(arg), axis=0))
        grown = jnp.exp2(t_arg[part, :] - t_top)
        t_sum = t_sum + jnp.sum(fold(grown), axis=0)
        half = grown.astype(bf16)
        ut_ref[part, :] = half
        t_acc = t_acc + jnp.dot(p_ref[:, part], half, preferred_element_type=f32)
    s_top = jnp.max(s_top, axis=0, keepdims=True)

    s_sum = jnp.zeros((8, rows), f32)
    s_acc = jnp.zeros((width, rows), f32)
    for part in chunks:
        grown = jnp.exp2(s_arg[part, :] - s_top)
        s_sum = s_sum + jnp.sum(fold(grown), axis=0)
        half = grown.astype(bf16)
        us_ref[part, :] = half
        s_acc = s_acc + jnp.dot(p_ref[:, part], half, preferred_element_type=f32)

    at_ref[...] = t_acc.T
    as_ref[...] = s_acc.T
    cross = jnp.sum(t_acc * s_rows.astype(f32).T, axis=0, keepdims=True)
    stat_ref[...] = jnp.concatenate(
        [
            t_top,
            jnp.sum(t_sum, axis=0, keepdims=True),
            cross,
            s_top,
            jnp.sum(s_sum, axis=0, keepdims=True),
            jnp.zeros((3, rows), f32),
        ],
        axis=0,
    )


def forward(s_half, t_half, protos_t, protos, shift):
    total, width = s_half.shape
    cols = protos.shape[1]
    block = 256
    whole = lambda shape: pl.BlockSpec(shape, lambda i: (0, 0))
    by_row = pl.BlockSpec((block, width), lambda i: (i, 0))
    by_lane = lambda height: pl.BlockSpec((height, block), lambda i: (0, i))
    return pl.pallas_call(
        forward_kernel,
        grid=(total // block,),
        in_specs=[by_row, by_row, whole((cols, width)), whole((width, cols)), whole(shift.shape)],
        out_specs=[by_lane(cols), by_lane(cols), by_row, by_row, by_lane(8)],
        out_shape=[
            jax.ShapeDtypeStruct((cols, total), bf16),
            jax.ShapeDtypeStruct((cols, total), bf16),
            jax.ShapeDtypeStruct((total, width), f32),
            jax.ShapeDtypeStruct((total, width), f32),
            jax.ShapeDtypeStruct((8, total), f32),
        ],
        scratch_shapes=[pltpu.VMEM((cols, block), f32)] * 2,
        compiler_params=pltpu.CompilerParams(vmem_limit_bytes=vmem_bytes),
        cost_estimate=pl.CostEstimate(
            flops=8 * total * width * cols,
            bytes_accessed=4 * total * cols,
            transcendentals=2 * total * cols,
        ),
        name="forward_rows",
    )(s_half, t_half, protos_t, protos, shift)


def proto_grad_kernel(us_ref, ut_ref, s_ref, t_ref, out_ref):
    out_ref[...] = jnp.dot(us_ref[...], s_ref[...], preferred_element_type=f32) - jnp.dot(
        ut_ref[...], t_ref[...], preferred_element_type=f32
    )


def proto_grad_call(us, ut, s_scaled, t_scaled):
    cols, total = us.shape
    width = s_scaled.shape[1]
    block = min(512, cols)
    tall = pl.BlockSpec((block, total), lambda i: (i, 0))
    whole = pl.BlockSpec((total, width), lambda i: (0, 0))
    return pl.pallas_call(
        proto_grad_kernel,
        grid=(cols // block,),
        in_specs=[tall, tall, whole, whole],
        out_specs=pl.BlockSpec((block, width), lambda i: (i, 0)),
        out_shape=jax.ShapeDtypeStruct((cols, width), f32),
        compiler_params=pltpu.CompilerParams(vmem_limit_bytes=vmem_bytes),
        cost_estimate=pl.CostEstimate(
            flops=4 * total * width * cols, bytes_accessed=4 * total * cols, transcendentals=0
        ),
        name="proto_grad_rows",
    )(us, ut, s_scaled, t_scaled)


def shards(student_rows, teacher_rows, prototypes, center, mask_index, mask_count, loss_scale):
    img_local, patches, width = student_rows.shape
    max_masked = mask_index.shape[1]
    data_size = lax.axis_size("dp")
    proto_size = lax.axis_size("proto")
    me_data = lax.axis_index("dp")
    me_proto = lax.axis_index("proto")
    images = img_local * data_size
    padded_rows = img_local * max_masked
    total = images * max_masked // 2
    cols = prototypes.shape[1] // data_size
    piece = padded_rows // proto_size

    patch_ids = jnp.arange(patches, dtype=jnp.int32)
    pick = (mask_index[:, :, None] == patch_ids).astype(bf16)
    both = jnp.concatenate([student_rows, teacher_rows], axis=2)
    picked = jnp.einsum("isp,ipd->isd", pick, both, preferred_element_type=f32)
    picked = picked.reshape(padded_rows, 2 * width)
    s_unit, s_len = unit_rows(picked[:, :width])
    t_unit, _ = unit_rows(picked[:, width:])
    halves = jnp.concatenate([s_unit.astype(bf16), t_unit.astype(bf16)], axis=1)

    mine = lax.dynamic_slice_in_dim(halves, me_proto * piece, piece, axis=0)
    counts_row = jnp.pad(mask_count.astype(bf16)[None, :], ((0, tail_rows - 1), (0, 2 * width - img_local)))
    sent = jnp.concatenate([mine, counts_row], axis=0)
    everyone = lax.all_gather(sent, ("dp", "proto"))
    counts = everyone[::proto_size, piece, :img_local].astype(jnp.int32).reshape(images)
    ends = jnp.cumsum(counts)
    starts = ends - counts
    s_half, t_half = compact(everyone, starts, max_masked, total, width)

    rank = jnp.arange(total, dtype=jnp.int32)[None, :]
    inside = (starts[:, None] <= rank) & (rank < ends[:, None])
    image_weight = 1.0 / (images * jnp.maximum(counts, 1).astype(f32))
    weight = jnp.sum(jnp.where(inside, image_weight[:, None], 0.0), axis=0)

    protos = lax.dynamic_slice_in_dim(prototypes, me_data * cols, cols, axis=1)
    my_center = lax.dynamic_slice_in_dim(center, me_data * cols, cols, axis=0)
    shift = jnp.broadcast_to((my_center * (log2_e / teacher_temp))[:, None], (cols, 128))
    us, ut, s_acc, t_acc, stats = forward(s_half, t_half, protos.T, protos, shift)

    all_stats = lax.all_gather(stats[:5], ("dp", "proto"))
    t_top, t_sum, cross, s_top, s_sum = (all_stats[:, k] for k in range(5))
    t_all = jnp.max(t_top, axis=0)
    s_all = jnp.max(s_top, axis=0)
    t_scale = jnp.exp2(t_top - t_all)
    t_total = jnp.sum(t_sum * t_scale, axis=0)
    s_total = jnp.sum(s_sum * jnp.exp2(s_top - s_all), axis=0)
    cross_mean = jnp.sum(cross * t_scale, axis=0) / t_total
    ce = ln_2 * (s_all + jnp.log2(s_total)) - cross_mean / student_temp
    loss = jnp.sum(weight * ce)

    coef = loss_scale * weight / student_temp
    s_factor = (coef * jnp.exp2(stats[3] - s_all) / s_total)[:, None]
    t_factor = (coef * jnp.exp2(stats[0] - t_all) / t_total)[:, None]
    d_part = (s_factor * s_acc - t_factor * t_acc).astype(bf16)
    d_all = lax.psum(d_part, ("dp", "proto"))

    s_wide = s_half.astype(f32)
    proto_grad = proto_grad_call(us, ut, (s_wide * s_factor).astype(bf16), (s_wide * t_factor).astype(bf16))

    t_rows_sum = jnp.sum(t_half.astype(f32), axis=0) / total
    high = lax.reduce_precision(t_rows_sum, 8, 7)
    rest = t_rows_sum - high
    middle = lax.reduce_precision(rest, 8, 7)
    parts = jnp.stack([high, middle, rest - middle]).astype(bf16)
    parts = jnp.pad(parts, ((0, 5), (0, 0)))
    patch_center = jnp.sum(jnp.dot(parts, prototypes, preferred_element_type=f32), axis=0)

    d_all = jnp.pad(d_all, ((0, max_masked), (0, 0)))
    my_starts = lax.dynamic_slice_in_dim(starts, me_data * img_local, img_local)
    d_unit = jnp.concatenate(
        [lax.dynamic_slice_in_dim(d_all, my_starts[i], max_masked, axis=0) for i in range(img_local)]
    ).astype(f32)
    row_grads = norm_backward(d_unit, s_unit, s_len).reshape(img_local, max_masked, width)
    slots = jnp.arange(max_masked, dtype=jnp.int32)
    valid = slots[None, :] < mask_count[:, None]
    place = (pick * valid[:, :, None].astype(bf16)).astype(f32)
    student_grad = jnp.einsum(
        "isp,isd->ipd", place, row_grads, precision=lax.Precision.HIGHEST, preferred_element_type=f32
    )
    return (loss, student_grad, proto_grad, patch_center)


def solution(mesh):
    in_specs = (
        P("dp", None, None),
        P("dp", None, None),
        P(None, "proto"),
        P("proto"),
        P("dp", None),
        P("dp"),
        P(),
    )
    out_specs = (P(), P("dp", None, None), P(("proto", "dp"), None), P("proto"))
    return jax.shard_map(shards, mesh=mesh, in_specs=in_specs, out_specs=out_specs, check_vma=False)
```

```python
import functools
import math

import jax
import jax.numpy as jnp
from jax import lax
from jax.experimental import pallas as pl
from jax.experimental.pallas import tpu as pltpu
from jax.sharding import PartitionSpec as P

teacher_temp = 0.04
student_temp = 0.1
norm_epsilon = 1e-06
log2_e = math.log2(math.e)
ln_2 = math.log(2.0)
tail_rows = 16
vmem_bytes = 56 * 1024 * 1024
f32 = jnp.float32
bf16 = jnp.bfloat16


def unit_rows(raw):
    values = raw.astype(f32)
    length = jnp.sqrt(jnp.sum(values * values, axis=1, keepdims=True) + norm_epsilon)
    return (values / length, length)


def norm_backward(d_unit, s_unit, s_len):
    return (d_unit - s_unit * jnp.sum(s_unit * d_unit, axis=1, keepdims=True)) / s_len


def compact_kernel(max_masked, starts_ref, rows_ref, s_ref, t_ref, held):
    devices, piece, both = rows_ref.shape
    piece -= tail_rows
    total, width = s_ref.shape
    chunk = min(piece, max_masked)

    @pl.loop(0, devices * piece // chunk)
    def _(step):
        flat = step * chunk
        image = flat // max_masked
        at = starts_ref[image] + flat % max_masked
        row = pl.multiple_of(flat % piece, chunk)
        base = pl.multiple_of(at // 8 * 8, 8)
        ahead = at - base
        value = rows_ref[flat // piece, pl.ds(row, chunk), :].astype(f32)
        value = jnp.concatenate([value, jnp.zeros((8, both), f32)], axis=0)
        value = pltpu.roll(value, ahead, 0)
        older = lax.broadcasted_iota(jnp.int32, (8, both), 0) < ahead
        held[pl.ds(base, 8), :] = jnp.where(older, held[pl.ds(base, 8), :], value[:8])
        held[pl.ds(pl.multiple_of(base + 8, 8), chunk), :] = value[8:]

    s_ref[...] = held[:total, :width].astype(bf16)
    t_ref[...] = held[:total, width:].astype(bf16)


def compact(rows, starts, max_masked, total, width):
    return pl.pallas_call(
        functools.partial(compact_kernel, max_masked),
        out_shape=[jax.ShapeDtypeStruct((total, width), bf16)] * 2,
        in_specs=[
            pl.BlockSpec(memory_space=pltpu.SMEM),
            pl.BlockSpec(memory_space=pltpu.VMEM),
        ],
        out_specs=[pl.BlockSpec(memory_space=pltpu.VMEM)] * 2,
        scratch_shapes=[pltpu.VMEM((total + max_masked + 8, 2 * width), f32)],
        compiler_params=pltpu.CompilerParams(vmem_limit_bytes=vmem_bytes),
        name="compact_rows",
    )(starts, rows)


def expand_kernel(max_masked, starts_ref, rows_ref, out_ref):
    tall = max_masked + 8

    @pl.loop(0, out_ref.shape[0] // max_masked)
    def _(image):
        at = starts_ref[image]
        base = pl.multiple_of(at // 8 * 8, 8)
        ahead = at - base
        value = rows_ref[pl.ds(base, tall), :]
        value = pltpu.roll(value, jnp.where(ahead == 0, 0, tall - ahead), 0)
        to = pl.multiple_of(image * max_masked, max_masked)
        out_ref[pl.ds(to, max_masked), :] = value[:max_masked].astype(bf16)


def expand(rows, starts, max_masked):
    return pl.pallas_call(
        functools.partial(expand_kernel, max_masked),
        out_shape=jax.ShapeDtypeStruct((starts.shape[0] * max_masked, rows.shape[1]), bf16),
        in_specs=[
            pl.BlockSpec(memory_space=pltpu.SMEM),
            pl.BlockSpec(memory_space=pltpu.VMEM),
        ],
        out_specs=pl.BlockSpec(memory_space=pltpu.VMEM),
        compiler_params=pltpu.CompilerParams(vmem_limit_bytes=vmem_bytes),
        name="expand_rows",
    )(starts, rows)


def merge_stats(stats):
    t_top, t_sum, cross, s_top, s_sum = (stats[:, k] for k in range(5))
    t_all = jnp.max(t_top, axis=0)
    s_all = jnp.max(s_top, axis=0)
    t_scale = jnp.exp2(t_top - t_all)
    return (
        t_all,
        jnp.sum(t_sum * t_scale, axis=0),
        jnp.sum(cross * t_scale, axis=0),
        s_all,
        jnp.sum(s_sum * jnp.exp2(s_top - s_all), axis=0),
    )


def nt_dot(left, right):
    return lax.dot_general(left, right, (((1,), (1,)), ((), ())), preferred_element_type=f32)


def forward_kernel(s_ref, t_ref, pt_ref, p_ref, c_ref, us_ref, ut_ref, as_ref, at_ref, stat_ref, s_arg, t_arg):
    cols, rows = s_arg.shape
    width = p_ref.shape[0]
    chunk = min(512, cols)
    chunks = [pl.ds(k * chunk, chunk) for k in range(cols // chunk)]
    s_rows = s_ref[...]
    t_rows = t_ref[...]
    lanes = c_ref.shape[1]

    def fold(value):
        return value.reshape(chunk // 8, 8, rows)

    t_top = jnp.full((8, rows), -jnp.inf, f32)
    for part in chunks:
        shift = jnp.concatenate([c_ref[part, :]] * (rows // lanes), axis=1)
        arg = nt_dot(pt_ref[part, :], t_rows) * (log2_e / teacher_temp) - shift
        t_arg[part, :] = arg
        t_top = jnp.maximum(t_top, jnp.max(fold(arg), axis=0))
    t_top = jnp.max(t_top, axis=0, keepdims=True)

    s_top = jnp.full((8, rows), -jnp.inf, f32)
    t_sum = jnp.zeros((8, rows), f32)
    t_acc = jnp.zeros((width, rows), f32)
    for part in chunks:
        arg = nt_dot(pt_ref[part, :], s_rows) * (log2_e / student_temp)
        s_arg[part, :] = arg
        s_top = jnp.maximum(s_top, jnp.max(fold(arg), axis=0))
        grown = jnp.exp2(t_arg[part, :] - t_top)
        t_sum = t_sum + jnp.sum(fold(grown), axis=0)
        half = grown.astype(bf16)
        ut_ref[part, :] = half
        t_acc = t_acc + jnp.dot(p_ref[:, part], half, preferred_element_type=f32)
    s_top = jnp.max(s_top, axis=0, keepdims=True)

    s_sum = jnp.zeros((8, rows), f32)
    s_acc = jnp.zeros((width, rows), f32)
    for part in chunks:
        grown = jnp.exp2(s_arg[part, :] - s_top)
        s_sum = s_sum + jnp.sum(fold(grown), axis=0)
        half = grown.astype(bf16)
        us_ref[part, :] = half
        s_acc = s_acc + jnp.dot(p_ref[:, part], half, preferred_element_type=f32)

    at_ref[...] = t_acc.T
    as_ref[...] = s_acc.T
    cross = jnp.sum(t_acc * s_rows.astype(f32).T, axis=0, keepdims=True)
    stat_ref[...] = jnp.concatenate(
        [
            t_top,
            jnp.sum(t_sum, axis=0, keepdims=True),
            cross,
            s_top,
            jnp.sum(s_sum, axis=0, keepdims=True),
            jnp.zeros((3, rows), f32),
        ],
        axis=0,
    )


def forward(s_half, t_half, protos_t, protos, shift):
    total, width = s_half.shape
    cols = protos.shape[1]
    block = 256
    whole = lambda shape: pl.BlockSpec(shape, lambda i: (0, 0))
    by_row = pl.BlockSpec((block, width), lambda i: (i, 0))
    by_lane = lambda height: pl.BlockSpec((height, block), lambda i: (0, i))
    return pl.pallas_call(
        forward_kernel,
        grid=(total // block,),
        in_specs=[by_row, by_row, whole((cols, width)), whole((width, cols)), whole(shift.shape)],
        out_specs=[by_lane(cols), by_lane(cols), by_row, by_row, by_lane(8)],
        out_shape=[
            jax.ShapeDtypeStruct((cols, total), bf16),
            jax.ShapeDtypeStruct((cols, total), bf16),
            jax.ShapeDtypeStruct((total, width), f32),
            jax.ShapeDtypeStruct((total, width), f32),
            jax.ShapeDtypeStruct((8, total), f32),
        ],
        scratch_shapes=[pltpu.VMEM((cols, block), f32)] * 2,
        compiler_params=pltpu.CompilerParams(vmem_limit_bytes=vmem_bytes),
        cost_estimate=pl.CostEstimate(
            flops=8 * total * width * cols,
            bytes_accessed=4 * total * cols,
            transcendentals=2 * total * cols,
        ),
        name="forward_rows",
    )(s_half, t_half, protos_t, protos, shift)


def proto_grad_kernel(us_ref, ut_ref, s_ref, t_ref, out_ref):
    out_ref[...] = jnp.dot(us_ref[...], s_ref[...], preferred_element_type=f32) - jnp.dot(
        ut_ref[...], t_ref[...], preferred_element_type=f32
    )


def proto_grad_call(us, ut, s_scaled, t_scaled):
    cols, total = us.shape
    width = s_scaled.shape[1]
    block = min(512, cols)
    tall = pl.BlockSpec((block, total), lambda i: (i, 0))
    whole = pl.BlockSpec((total, width), lambda i: (0, 0))
    return pl.pallas_call(
        proto_grad_kernel,
        grid=(cols // block,),
        in_specs=[tall, tall, whole, whole],
        out_specs=pl.BlockSpec((block, width), lambda i: (i, 0)),
        out_shape=jax.ShapeDtypeStruct((cols, width), f32),
        compiler_params=pltpu.CompilerParams(vmem_limit_bytes=vmem_bytes),
        cost_estimate=pl.CostEstimate(
            flops=4 * total * width * cols, bytes_accessed=4 * total * cols, transcendentals=0
        ),
        name="proto_grad_rows",
    )(us, ut, s_scaled, t_scaled)


def shards(student_rows, teacher_rows, prototypes, center, mask_index, mask_count, loss_scale):
    img_local, patches, width = student_rows.shape
    max_masked = mask_index.shape[1]
    data_size = lax.axis_size("dp")
    me_data = lax.axis_index("dp")
    images = img_local * data_size
    padded_rows = img_local * max_masked
    total = images * max_masked // 2
    cols = prototypes.shape[1] // data_size

    patch_ids = jnp.arange(patches, dtype=jnp.int32)
    pick = (mask_index[:, :, None] == patch_ids).astype(bf16)
    both = jnp.concatenate([student_rows, teacher_rows], axis=2)
    picked = jnp.einsum("isp,ipd->isd", pick, both, preferred_element_type=f32)
    picked = picked.reshape(padded_rows, 2 * width)
    s_unit, s_len = unit_rows(picked[:, :width])
    t_unit, _ = unit_rows(picked[:, width:])
    halves = jnp.concatenate([s_unit.astype(bf16), t_unit.astype(bf16)], axis=1)

    counts_row = jnp.pad(mask_count.astype(bf16)[None, :], ((0, tail_rows - 1), (0, 2 * width - img_local)))
    sent = jnp.concatenate([halves, counts_row], axis=0)
    everyone = lax.all_gather(sent, "dp")
    counts = everyone[:, padded_rows, :img_local].astype(jnp.int32).reshape(images)
    ends = jnp.cumsum(counts)
    starts = ends - counts
    s_half, t_half = compact(everyone, starts, max_masked, total, width)

    rank = jnp.arange(total, dtype=jnp.int32)[None, :]
    inside = (starts[:, None] <= rank) & (rank < ends[:, None])
    image_weight = 1.0 / (images * jnp.maximum(counts, 1).astype(f32))
    weight = jnp.sum(jnp.where(inside, image_weight[:, None], 0.0), axis=0)

    protos = lax.dynamic_slice_in_dim(prototypes, me_data * cols, cols, axis=1)
    my_center = lax.dynamic_slice_in_dim(center, me_data * cols, cols, axis=0)
    shift = jnp.broadcast_to((my_center * (log2_e / teacher_temp))[:, None], (cols, 128))
    us, ut, s_acc, t_acc, stats = forward(s_half, t_half, protos.T, protos, shift)

    merged = merge_stats(lax.all_gather(stats[:5], "proto"))
    t_all, t_total, cross, s_all, s_total = merge_stats(lax.all_gather(jnp.stack(merged), "dp"))
    cross_mean = cross / t_total
    ce = ln_2 * (s_all + jnp.log2(s_total)) - cross_mean / student_temp
    loss = jnp.sum(weight * ce)

    coef = loss_scale * weight / student_temp
    s_factor = (coef * jnp.exp2(stats[3] - s_all) / s_total)[:, None]
    t_factor = (coef * jnp.exp2(stats[0] - t_all) / t_total)[:, None]
    d_part = jnp.pad(s_factor * s_acc - t_factor * t_acc, ((0, max_masked + 8), (0, 0)))
    d_slots = expand(d_part, starts, max_masked)
    d_mine = lax.psum_scatter(d_slots, "dp", scatter_dimension=0, tiled=True)

    s_wide = s_half.astype(f32)
    proto_grad = proto_grad_call(us, ut, (s_wide * s_factor).astype(bf16), (s_wide * t_factor).astype(bf16))

    t_rows_sum = jnp.sum(t_half.astype(f32), axis=0) / total
    high = lax.reduce_precision(t_rows_sum, 8, 7)
    rest = t_rows_sum - high
    middle = lax.reduce_precision(rest, 8, 7)
    parts = jnp.stack([high, middle, rest - middle]).astype(bf16)
    parts = jnp.pad(parts, ((0, 5), (0, 0)))
    patch_center = jnp.sum(jnp.dot(parts, prototypes, preferred_element_type=f32), axis=0)

    d_unit = lax.psum(d_mine, "proto").astype(f32)
    row_grads = norm_backward(d_unit, s_unit, s_len).reshape(img_local, max_masked, width)
    slots = jnp.arange(max_masked, dtype=jnp.int32)
    valid = slots[None, :] < mask_count[:, None]
    place = (pick * valid[:, :, None].astype(bf16)).astype(f32)
    student_grad = jnp.einsum(
        "isp,isd->ipd", place, row_grads, precision=lax.Precision.HIGHEST, preferred_element_type=f32
    )
    return (loss, student_grad, proto_grad, patch_center)


def solution(mesh):
    in_specs = (
        P("dp", None, None),
        P("dp", None, None),
        P(None, "proto"),
        P("proto"),
        P("dp", None),
        P("dp"),
        P(),
    )
    out_specs = (P(), P("dp", None, None), P(("proto", "dp"), None), P("proto"))
    return jax.shard_map(shards, mesh=mesh, in_specs=in_specs, out_specs=out_specs, check_vma=False)
```

```python
import functools
import math

import jax
import jax.numpy as jnp
from jax import lax
from jax.experimental import pallas as pl
from jax.experimental.pallas import tpu as pltpu
from jax.sharding import PartitionSpec as P

teacher_temp = 0.04
student_temp = 0.1
norm_epsilon = 1e-06
log2_e = math.log2(math.e)
ln_2 = math.log(2.0)
tail_rows = 16
vmem_bytes = 56 * 1024 * 1024
f32 = jnp.float32
bf16 = jnp.bfloat16


def unit_rows(raw):
    values = raw.astype(f32)
    length = jnp.sqrt(jnp.sum(values * values, axis=1, keepdims=True) + norm_epsilon)
    return (values / length, length)


def norm_backward(d_unit, s_unit, s_len):
    return (d_unit - s_unit * jnp.sum(s_unit * d_unit, axis=1, keepdims=True)) / s_len


def compact_kernel(max_masked, starts_ref, rows_ref, s_ref, t_ref, held):
    devices, piece, both = rows_ref.shape
    piece -= tail_rows
    total, width = s_ref.shape
    chunk = min(piece, max_masked)

    @pl.loop(0, devices * piece // chunk)
    def _(step):
        flat = step * chunk
        image = flat // max_masked
        at = starts_ref[image] + flat % max_masked
        row = pl.multiple_of(flat % piece, chunk)
        base = pl.multiple_of(at // 8 * 8, 8)
        ahead = at - base
        value = rows_ref[flat // piece, pl.ds(row, chunk), :].astype(f32)
        value = jnp.concatenate([value, jnp.zeros((8, both), f32)], axis=0)
        value = pltpu.roll(value, ahead, 0)
        older = lax.broadcasted_iota(jnp.int32, (8, both), 0) < ahead
        held[pl.ds(base, 8), :] = jnp.where(older, held[pl.ds(base, 8), :], value[:8])
        held[pl.ds(pl.multiple_of(base + 8, 8), chunk), :] = value[8:]

    s_ref[...] = held[:total, :width].astype(bf16)
    t_ref[...] = held[:total, width:].astype(bf16)


def compact(rows, starts, max_masked, total, width):
    return pl.pallas_call(
        functools.partial(compact_kernel, max_masked),
        out_shape=[jax.ShapeDtypeStruct((total, width), bf16)] * 2,
        in_specs=[
            pl.BlockSpec(memory_space=pltpu.SMEM),
            pl.BlockSpec(memory_space=pltpu.VMEM),
        ],
        out_specs=[pl.BlockSpec(memory_space=pltpu.VMEM)] * 2,
        scratch_shapes=[pltpu.VMEM((total + max_masked + 8, 2 * width), f32)],
        compiler_params=pltpu.CompilerParams(vmem_limit_bytes=vmem_bytes),
        name="compact_rows",
    )(starts, rows)


def expand_kernel(max_masked, starts_ref, rows_ref, out_ref):
    tall = max_masked + 8

    @pl.loop(0, out_ref.shape[0] // max_masked)
    def _(image):
        at = starts_ref[image]
        base = pl.multiple_of(at // 8 * 8, 8)
        ahead = at - base
        value = rows_ref[pl.ds(base, tall), :]
        value = pltpu.roll(value, jnp.where(ahead == 0, 0, tall - ahead), 0)
        to = pl.multiple_of(image * max_masked, max_masked)
        out_ref[pl.ds(to, max_masked), :] = value[:max_masked].astype(bf16)


def expand(rows, starts, max_masked):
    return pl.pallas_call(
        functools.partial(expand_kernel, max_masked),
        out_shape=jax.ShapeDtypeStruct((starts.shape[0] * max_masked, rows.shape[1]), bf16),
        in_specs=[
            pl.BlockSpec(memory_space=pltpu.SMEM),
            pl.BlockSpec(memory_space=pltpu.VMEM),
        ],
        out_specs=pl.BlockSpec(memory_space=pltpu.VMEM),
        compiler_params=pltpu.CompilerParams(vmem_limit_bytes=vmem_bytes),
        name="expand_rows",
    )(starts, rows)


def merge_stats(stats):
    t_top, t_sum, cross, s_top, s_sum = (stats[:, k] for k in range(5))
    t_all = jnp.max(t_top, axis=0)
    s_all = jnp.max(s_top, axis=0)
    t_scale = jnp.exp2(t_top - t_all)
    return (
        t_all,
        jnp.sum(t_sum * t_scale, axis=0),
        jnp.sum(cross * t_scale, axis=0),
        s_all,
        jnp.sum(s_sum * jnp.exp2(s_top - s_all), axis=0),
    )


def nt_dot(left, right):
    return lax.dot_general(left, right, (((1,), (1,)), ((), ())), preferred_element_type=f32)


def forward_kernel(s_ref, t_ref, pt_ref, p_ref, c_ref, us_ref, ut_ref, as_ref, at_ref, stat_ref, s_arg, t_arg):
    cols, rows = s_arg.shape
    width = p_ref.shape[0]
    chunk = min(512, cols)
    chunks = [pl.ds(k * chunk, chunk) for k in range(cols // chunk)]
    s_rows = s_ref[...]
    t_rows = t_ref[...]
    lanes = c_ref.shape[1]

    def fold(value):
        return value.reshape(chunk // 8, 8, rows)

    t_top = jnp.full((8, rows), -jnp.inf, f32)
    for part in chunks:
        shift = jnp.concatenate([c_ref[part, :]] * (rows // lanes), axis=1)
        arg = nt_dot(pt_ref[part, :], t_rows) * (log2_e / teacher_temp) - shift
        t_arg[part, :] = arg
        t_top = jnp.maximum(t_top, jnp.max(fold(arg), axis=0))
    t_top = jnp.max(t_top, axis=0, keepdims=True)

    s_top = jnp.full((8, rows), -jnp.inf, f32)
    t_sum = jnp.zeros((8, rows), f32)
    t_acc = jnp.zeros((width, rows), f32)
    for part in chunks:
        arg = nt_dot(pt_ref[part, :], s_rows) * (log2_e / student_temp)
        s_arg[part, :] = arg
        s_top = jnp.maximum(s_top, jnp.max(fold(arg), axis=0))
        grown = jnp.exp2(t_arg[part, :] - t_top)
        t_sum = t_sum + jnp.sum(fold(grown), axis=0)
        half = grown.astype(bf16)
        ut_ref[part, :] = half
        t_acc = t_acc + jnp.dot(p_ref[:, part], half, preferred_element_type=f32)
    s_top = jnp.max(s_top, axis=0, keepdims=True)

    s_sum = jnp.zeros((8, rows), f32)
    s_acc = jnp.zeros((width, rows), f32)
    for part in chunks:
        grown = jnp.exp2(s_arg[part, :] - s_top)
        s_sum = s_sum + jnp.sum(fold(grown), axis=0)
        half = grown.astype(bf16)
        us_ref[part, :] = half
        s_acc = s_acc + jnp.dot(p_ref[:, part], half, preferred_element_type=f32)

    at_ref[...] = t_acc.T
    as_ref[...] = s_acc.T
    cross = jnp.sum(t_acc * s_rows.astype(f32).T, axis=0, keepdims=True)
    stat_ref[...] = jnp.concatenate(
        [
            t_top,
            jnp.sum(t_sum, axis=0, keepdims=True),
            cross,
            s_top,
            jnp.sum(s_sum, axis=0, keepdims=True),
            jnp.zeros((3, rows), f32),
        ],
        axis=0,
    )


def forward(s_half, t_half, protos_t, protos, shift):
    total, width = s_half.shape
    cols = protos.shape[1]
    block = 256
    whole = lambda shape: pl.BlockSpec(shape, lambda i: (0, 0))
    by_row = pl.BlockSpec((block, width), lambda i: (i, 0))
    by_lane = lambda height: pl.BlockSpec((height, block), lambda i: (0, i))
    return pl.pallas_call(
        forward_kernel,
        grid=(total // block,),
        in_specs=[by_row, by_row, whole((cols, width)), whole((width, cols)), whole(shift.shape)],
        out_specs=[by_lane(cols), by_lane(cols), by_row, by_row, by_lane(8)],
        out_shape=[
            jax.ShapeDtypeStruct((cols, total), bf16),
            jax.ShapeDtypeStruct((cols, total), bf16),
            jax.ShapeDtypeStruct((total, width), f32),
            jax.ShapeDtypeStruct((total, width), f32),
            jax.ShapeDtypeStruct((8, total), f32),
        ],
        scratch_shapes=[pltpu.VMEM((cols, block), f32)] * 2,
        compiler_params=pltpu.CompilerParams(vmem_limit_bytes=vmem_bytes),
        cost_estimate=pl.CostEstimate(
            flops=8 * total * width * cols,
            bytes_accessed=4 * total * cols,
            transcendentals=2 * total * cols,
        ),
        name="forward_rows",
    )(s_half, t_half, protos_t, protos, shift)


def proto_grad_kernel(us_ref, ut_ref, s_ref, t_ref, out_ref):
    out_ref[...] = jnp.dot(us_ref[...], s_ref[...], preferred_element_type=f32) - jnp.dot(
        ut_ref[...], t_ref[...], preferred_element_type=f32
    )


def proto_grad_call(us, ut, s_scaled, t_scaled):
    cols, total = us.shape
    width = s_scaled.shape[1]
    block = min(512, cols)
    tall = pl.BlockSpec((block, total), lambda i: (i, 0))
    whole = pl.BlockSpec((total, width), lambda i: (0, 0))
    return pl.pallas_call(
        proto_grad_kernel,
        grid=(cols // block,),
        in_specs=[tall, tall, whole, whole],
        out_specs=pl.BlockSpec((block, width), lambda i: (i, 0)),
        out_shape=jax.ShapeDtypeStruct((cols, width), f32),
        compiler_params=pltpu.CompilerParams(vmem_limit_bytes=vmem_bytes),
        cost_estimate=pl.CostEstimate(
            flops=4 * total * width * cols, bytes_accessed=4 * total * cols, transcendentals=0
        ),
        name="proto_grad_rows",
    )(us, ut, s_scaled, t_scaled)


def shards(student_rows, teacher_rows, prototypes, center, mask_index, mask_count, loss_scale):
    img_local, patches, width = student_rows.shape
    max_masked = mask_index.shape[1]
    data_size = lax.axis_size("dp")
    me_data = lax.axis_index("dp")
    images = img_local * data_size
    padded_rows = img_local * max_masked
    total = images * max_masked // 2
    cols = prototypes.shape[1] // data_size

    patch_ids = jnp.arange(patches, dtype=jnp.int32)
    pick = (mask_index[:, :, None] == patch_ids).astype(bf16)
    both = jnp.concatenate([student_rows, teacher_rows], axis=2)
    picked = jnp.einsum("isp,ipd->isd", pick, both, preferred_element_type=f32)
    picked = picked.reshape(padded_rows, 2 * width)
    s_unit, s_len = unit_rows(picked[:, :width])
    t_unit, _ = unit_rows(picked[:, width:])
    halves = jnp.concatenate([s_unit.astype(bf16), t_unit.astype(bf16)], axis=1)

    counts_row = jnp.pad(mask_count.astype(bf16)[None, :], ((0, tail_rows - 1), (0, 2 * width - img_local)))
    sent = jnp.concatenate([halves, counts_row], axis=0)
    everyone = lax.all_gather(sent, "dp")
    counts = everyone[:, padded_rows, :img_local].astype(jnp.int32).reshape(images)
    ends = jnp.cumsum(counts)
    starts = ends - counts
    s_half, t_half = compact(everyone, starts, max_masked, total, width)

    rank = jnp.arange(total, dtype=jnp.int32)[None, :]
    inside = (starts[:, None] <= rank) & (rank < ends[:, None])
    image_weight = 1.0 / (images * jnp.maximum(counts, 1).astype(f32))
    weight = jnp.sum(jnp.where(inside, image_weight[:, None], 0.0), axis=0)

    protos = lax.dynamic_slice_in_dim(prototypes, me_data * cols, cols, axis=1)
    my_center = lax.dynamic_slice_in_dim(center, me_data * cols, cols, axis=0)
    shift = jnp.broadcast_to((my_center * (log2_e / teacher_temp))[:, None], (cols, 128))
    us, ut, s_acc, t_acc, stats = forward(s_half, t_half, protos.T, protos, shift)

    merged = merge_stats(lax.all_gather(stats[:5], "proto"))
    t_all, t_total, cross, s_all, s_total = merge_stats(lax.all_gather(jnp.stack(merged), "dp"))
    cross_mean = cross / t_total
    ce = ln_2 * (s_all + jnp.log2(s_total)) - cross_mean / student_temp
    loss = jnp.sum(weight * ce)

    coef = loss_scale * weight / student_temp
    s_factor = (coef * jnp.exp2(stats[3] - s_all) / s_total)[:, None]
    t_factor = (coef * jnp.exp2(stats[0] - t_all) / t_total)[:, None]
    d_part = jnp.pad(s_factor * s_acc - t_factor * t_acc, ((0, max_masked + 8), (0, 0)))
    d_slots = expand(d_part, starts, max_masked)
    d_mine = lax.psum_scatter(d_slots, "dp", scatter_dimension=0, tiled=True)

    s_wide = s_half.astype(f32)
    proto_grad = proto_grad_call(us, ut, (s_wide * s_factor).astype(bf16), (s_wide * t_factor).astype(bf16))

    t_rows_sum = jnp.sum(t_half.astype(f32), axis=0) / total
    high = lax.reduce_precision(t_rows_sum, 8, 7)
    rest = t_rows_sum - high
    middle = lax.reduce_precision(rest, 8, 7)
    parts = jnp.stack([high, middle, rest - middle]).astype(bf16)
    parts = jnp.pad(parts, ((0, 5), (0, 0)))
    patch_center = jnp.sum(jnp.dot(parts, prototypes, preferred_element_type=f32), axis=0)

    d_unit = lax.psum(d_mine.astype(f32), "proto")
    row_grads = norm_backward(d_unit, s_unit, s_len).reshape(img_local, max_masked, width)
    slots = jnp.arange(max_masked, dtype=jnp.int32)
    valid = slots[None, :] < mask_count[:, None]
    place = (pick * valid[:, :, None].astype(bf16)).astype(f32)
    student_grad = jnp.einsum(
        "isp,isd->ipd", place, row_grads, precision=lax.Precision.HIGHEST, preferred_element_type=f32
    )
    return (loss, student_grad, proto_grad, patch_center)


def solution(mesh):
    in_specs = (
        P("dp", None, None),
        P("dp", None, None),
        P(None, "proto"),
        P("proto"),
        P("dp", None),
        P("dp"),
        P(),
    )
    out_specs = (P(), P("dp", None, None), P(("proto", "dp"), None), P("proto"))
    return jax.shard_map(shards, mesh=mesh, in_specs=in_specs, out_specs=out_specs, check_vma=False)
```
